32 devices in a mesh: section: 4 (over x, core), dp: 8 (over z, y).
Axes of the slice: x: 2, y: 2, z: 4, core: 2. Of those that a mesh axis runs over, the one named last changes fastest.
Arguments:
- item_owner: int32 [4, 8, 128, 1], P('section', 'dp'), may hold values from 0 to 7; in each aligned block of 128 rows (0 to 127, 128 to 255, ..., all dimensions but the last counted through in order) at most 32 rows name the same one
- item_row: int32 [4, 8, 128], P('section', 'dp'), may hold values from 0 to 255
- lengths: int32 [4, 8], P(None, 'dp'), may hold values from 1 to 128
- table: bfloat16 [2048, 1024], P('dp'), may hold values from -6 to 6
- w_in: bfloat16 [4, 1024, 4096], P('section', 'dp'), may hold values from -0.1875 to 0.1875
- w_out: bfloat16 [4, 1024, 1024], P('section', 'dp'), may hold values from -0.1875 to 0.1875
- gain_in: float32 [4, 1024], P('section'), may hold values from 0.5 to 1.5
- gain_mid: float32 [4, 1024], P('section'), may hold values from 0.5 to 1.5
Outputs:
- states: bfloat16 [4, 8, 4, 128, 1024], P('section', 'dp')
The draws below stay inside these ranges and needn't reach their ends.
Inputs may be any that keep to these rules, and one draw needn't show every extreme that they name: Among the 128 events of one history no value of item_owner appears more than 32 times; some history reaches 32.
All inputs are finite; a program needn't handle non-finite values.
Results may differ from the reference program's by a relative error of at most 0.029.
Values may be sent and summed in bfloat16 or wider, within the bound.
A program may use at most 64 MiB of HBM per device.

```python
import math
import jax
import jax.numpy as jnp
import numpy as np
from jax import lax

D = 1024
HEADS = 8
HEAD_DIM = 128
LEN = 128
ROWS_DEV = 256
MICRO = 4
GROUPS = 8
ITEMS = 2048
CAP = 32
N_SECTION = 4
N_DP = 8


def set_ends(values, rng, smallest, top_value):
    longest = values.shape.index(max(values.shape))
    spots = []
    for shift in (0, 1):
        where = [jax.random.randint(jax.random.fold_in(rng, axis), (), 0, length) for axis, length in enumerate(values.shape)]
        where[longest] = (where[longest] + shift) % values.shape[longest]
        spots.append(tuple(where))
    return values.at[spots[0]].set(smallest).at[spots[1]].set(top_value)


def block_scale(key, dims, shards, low, high):
    factor_of, own = 1.0, jax.random.fold_in(key, 6)
    for dim, shards_of in shards:
        draws = jnp.exp(jax.random.uniform(jax.random.fold_in(own, dim), (shards_of,), jnp.float32, low / len(shards), high / len(shards)))
        factor_of = factor_of * jnp.repeat(draws, dims[dim] // shards_of).reshape([-1 if axis == dim else 1 for axis in range(len(dims))])
    return factor_of


def shared_out(key, own, number, rows, number_of, top, limit, lean):
    order = jax.random.permutation(key, number_of)
    packed, common = load_shares(number_of, rows * top, limit, lean, True), load_shares(number_of, rows * top, limit, lean, False)
    places = jnp.arange(number_of)

    def named(sizes, offset_by):
        used = int((sizes > 0).sum())
        fixed = max(1, used // 4)
        shifted = fixed + (places - fixed + offset_by * (used - fixed)) % max(1, number_of - fixed)
        return jnp.zeros((number_of,), jnp.int32).at[order[jnp.where(places < fixed, places, shifted)]].set(jnp.asarray(sizes, jnp.int32))

    sizes = jnp.where(number % 4 == 0, named(packed, number // 4), named(common, number - number // 4 - 1))
    mixed = jax.random.permutation(jax.random.fold_in(own, 3), number_of)
    giver, sink = mixed[0:number_of // 2 * 2:2], mixed[1:number_of // 2 * 2:2]
    slack = jnp.minimum(sizes[giver] - 1, limit - sizes[sink]) // 2
    slack = jnp.where((giver == order[0]) | (sink == order[0]) | (sizes[sink] == 0), 0, jnp.maximum(slack, 0))
    shifted = jax.random.randint(jax.random.fold_in(own, 4), (number_of // 2,), 0, 1 << 20) % (slack + 1)
    sizes = sizes.at[giver].add(-shifted).at[sink].add(shifted)
    items = jnp.searchsorted(jnp.cumsum(sizes), jnp.arange(rows * top), side="right").astype(jnp.int32)
    listing = items.reshape(top, rows).T
    listing = listing[jax.random.permutation(jax.random.fold_in(own, 1), rows)]
    offset_by = jax.random.randint(jax.random.fold_in(own, 2), (rows, 1), 0, top)
    return jnp.take_along_axis(listing, (jnp.arange(top)[None, :] + offset_by) % top, axis=1)


def load_shares(count, total, limit, lean, full):
    loads = [(1 << 20) // math.isqrt(standing ** lean) + 1 for standing in range(1, count + 1)]
    largest = limit if full else min(limit, max(-(-total // count), total * loads[0] // sum(loads)))
    least = 1 if total - largest >= count - 1 else 0
    counts, surplus = [largest] + [least] * (count - 1), total - largest - least * (count - 1)
    while surplus > 0:
        candidates = [i for i in range(1, count) if counts[i] < largest] or [i for i in range(1, count) if counts[i] < limit]
        pool, left = sum([loads[i] for i in candidates]), surplus
        for i in candidates:
            addition = min(limit - counts[i], max(1, left * loads[i] // pool), surplus)
            counts[i] = counts[i] + addition
            surplus = surplus - addition
    return np.array(counts)


def scatter_about(own_key, dims, width, bound, shards=(), kind=jnp.bfloat16):
    values = jax.random.normal(own_key, dims, jnp.float32) * width
    if len(shards) > 0:
        values = block_scale(own_key, dims, shards, -0.22, 0.18) * values
    return jnp.clip(values, min=-bound, max=bound).astype(kind)


def setup_inputs(seed: int = 0) -> dict:
    key_list = jax.random.split(jax.random.key(seed), 9)
    item_owner_keys = jax.random.split(jax.random.fold_in(key_list[0], 1), MICRO * GROUPS * LEN // LEN)
    item_owner_turns = jax.random.permutation(jax.random.fold_in(key_list[0], 3), MICRO * GROUPS * LEN // LEN)
    item_owner = jax.vmap(lambda own, number: shared_out(jax.random.fold_in(key_list[0], 2), own, number, LEN, N_DP, 1, CAP, 1))(item_owner_keys, item_owner_turns).reshape((MICRO, GROUPS, LEN, 1))
    item_row = set_ends(jax.random.randint(key_list[1], (MICRO, GROUPS, LEN), 0, ROWS_DEV), jax.random.fold_in(key_list[1], 1), 0, ROWS_DEV - 1).astype(jnp.int32)
    lengths = set_ends(jax.random.randint(key_list[2], (MICRO, GROUPS), 1, LEN + 1), jax.random.fold_in(key_list[2], 1), 1, LEN).astype(jnp.int32)
    table = scatter_about(key_list[3], (ITEMS, D), 1.0, 6.0, ((0, 8),))
    w_in = scatter_about(key_list[4], (N_SECTION, D, 4 * D), D ** -0.5, 0.1875, ((0, 4), (1, 8)))
    w_out = scatter_about(key_list[5], (N_SECTION, D, D), D ** -0.5, 0.1875, ((0, 4), (1, 8)))
    gain_in = jnp.clip(1.0 + 0.1 * jax.random.normal(key_list[6], (N_SECTION, D), jnp.float32), 0.5, 1.5)
    gain_mid = jnp.clip(1.0 + 0.1 * jax.random.normal(key_list[7], (N_SECTION, D), jnp.float32), 0.5, 1.5)
    return dict(item_owner=item_owner, item_row=item_row, lengths=lengths, table=table, w_in=w_in, w_out=w_out, gain_in=gain_in, gain_mid=gain_mid)


EPS = 1e-05

def normalize(values):
    center = values - lax.optimization_barrier(jnp.mean(values, axis=-1, keepdims=True))
    spread = lax.optimization_barrier(jnp.mean(center * center, axis=-1, keepdims=True))
    return center * lax.rsqrt(spread + EPS)

def hstu_layer(current, length, weight_in, weight_out, scale_in, scale_mid):
    wide = current.astype(jnp.float32)
    normed = (normalize(wide) * scale_in).astype(jnp.bfloat16)
    uvqk = jax.nn.silu(jnp.dot(normed, weight_in, preferred_element_type=jnp.float32)).astype(jnp.bfloat16)
    u_part, v_part, q_part, k_part = jnp.split(uvqk, 4, axis=-1)
    rows = current.shape[0]
    queries = q_part.reshape(rows, HEADS, HEAD_DIM).astype(jnp.float32)
    keys = k_part.reshape(rows, HEADS, HEAD_DIM).astype(jnp.float32)
    values = v_part.reshape(rows, HEADS, HEAD_DIM).astype(jnp.float32)
    scores = jnp.einsum('qhd,khd->hqk', queries, keys)
    position = jnp.arange(rows, dtype=jnp.int32)
    allowed = (position[None, :] <= position[:, None]) & (position[None, :] < length)
    weights = jnp.where(allowed[None], jax.nn.silu(scores / jnp.sqrt(jnp.float32(HEAD_DIM))), 0.0).astype(jnp.bfloat16)
    attn = jnp.einsum('hqk,khd->qhd', weights.astype(jnp.float32), values).reshape(rows, HEADS * HEAD_DIM)
    mixed = (normalize(attn) * scale_mid * u_part.astype(jnp.float32)).astype(jnp.bfloat16)
    return (jnp.dot(mixed, weight_out, preferred_element_type=jnp.float32) + wide).astype(jnp.bfloat16)

def reference(item_owner, item_row, lengths, table, w_in, w_out, gain_in, gain_mid):
    sections = w_in.shape[0]
    micro, groups, seq_len = item_row.shape
    index = (item_owner[..., 0] * ROWS_DEV + item_row).astype(jnp.int32).reshape(micro * groups, seq_len)
    lens = lengths.reshape(micro * groups).astype(jnp.int32)

    def one_history(pair):
        rows, length = pair
        current = jnp.take(table, rows, axis=0)
        kept = []
        for level in range(sections):
            current = hstu_layer(current, length, w_in[level], w_out[level], gain_in[level], gain_mid[level])
            kept.append(current)
        return jnp.stack(kept)
    result = lax.map(one_history, (index, lens))
    result = result.reshape(micro, groups, sections, seq_len, table.shape[1])
    return jnp.transpose(result, (2, 1, 0, 3, 4))
```

```python
import functools

import jax
import jax.numpy as jnp
from jax import lax
from jax.experimental import pallas as pl
from jax.experimental.pallas import tpu as pltpu
from jax.sharding import PartitionSpec as P

HEADS = 8
EPS = 1e-05
MESH = pl.DeviceIdType.MESH
SUBLANES = 8
PACKED_ROWS = 16


def dot(a, b, contract=(1, 0)):
    dims = (((contract[0],), (contract[1],)), ((), ()))
    return lax.dot_general(a, b, dims, preferred_element_type=jnp.float32)


def silu(v):
    half = 0.5 * v
    return half + half * jnp.tanh(half)


def normalize(values):
    center = values - jnp.mean(values, axis=-1, keepdims=True)
    spread = jnp.mean(center * center, axis=-1, keepdims=True)
    return center * lax.rsqrt(spread + EPS)


def kernel(
    lines,
    lens_ref, code_ref, table_ref, w_in_ref, w_out_ref, gain_in_ref, gain_mid_ref,
    out_ref,
    win, wout, codes, answers, found, staged, xin, normed, uvqk, attn,
    local_sem, win_send, win_recv, wout_send, wout_recv,
    code_send, code_recv, found_send, found_recv, x_send, x_recv, next_send,
):
    major, minor = lines
    groups = major * minor
    here, me = lax.axis_index("section"), lax.axis_index("dp")
    sections = lax.axis_size("section")
    a, b = me // minor, me % minor
    depth, depth_out = w_in_ref.shape[0], w_out_ref.shape[0]
    micro, seq, width = xin.shape
    cap = answers.shape[1]
    items = table_ref.shape[0]
    head = width // HEADS

    def rows(ref, block, count):
        return ref.at[pl.ds(pl.multiple_of(block * count, count), count)]

    def target(kind):
        if kind == 0:
            return (a + 1) * minor + b
        if kind == 1:
            return (a - 1) * minor + b
        return a * minor + (b + kind - 1) % minor

    def weight_copy(which, block, kind):
        full, send, recv, count = (
            (win, win_send, win_recv, depth) if which == 0 else (wout, wout_send, wout_recv, depth_out)
        )
        part = rows(full, block, count)
        return pltpu.make_async_remote_copy(
            src_ref=part, dst_ref=part, send_sem=send.at[block, kind], recv_sem=recv.at[block],
            device_id={"dp": target(kind)}, device_id_type=MESH,
        )

    def code_copy(block, to):
        return pltpu.make_async_remote_copy(
            src_ref=codes.at[block], dst_ref=codes.at[block], send_sem=code_send.at[to],
            recv_sem=code_recv.at[block], device_id={"dp": to}, device_id_type=MESH,
        )

    def found_copy(to, block):
        return pltpu.make_async_remote_copy(
            src_ref=answers.at[to], dst_ref=found.at[block], send_sem=found_send.at[to],
            recv_sem=found_recv.at[block], device_id={"dp": to}, device_id_type=MESH,
        )

    def to_first(slot):
        return pltpu.make_async_remote_copy(
            src_ref=staged, dst_ref=xin.at[slot], send_sem=x_send.at[0], recv_sem=x_recv.at[slot],
            device_id={"section": 0}, device_id_type=MESH,
        )

    def to_next(slot):
        return pltpu.make_async_remote_copy(
            src_ref=out_ref.at[slot], dst_ref=xin.at[slot], send_sem=next_send.at[slot],
            recv_sem=x_recv.at[slot], device_id={"section": here + 1}, device_id_type=MESH,
        )

    UP, DOWN = 0, 1
    ACROSS = range(2, minor + 1)

    def other(off):
        return a * minor + (b + off) % minor

    def start_if(copy, condition):
        if condition is None:
            copy.start()
        else:
            pl.when(condition)(copy.start)

    own_in = pltpu.make_async_copy(w_in_ref, rows(win, me, depth), local_sem.at[0])
    own_out = pltpu.make_async_copy(w_out_ref, rows(wout, me, depth_out), local_sem.at[1])
    own_in.start()
    own_out.start()
    codes[me] = jnp.broadcast_to(code_ref[...], codes.shape[1:])

    def send_code(off, _):
        code_copy(me, lax.rem(me + off, groups)).start()
        return 0

    lax.fori_loop(1, groups, send_code, 0)
    own_out.wait()
    own_in.wait()
    for which in (1, 0):
        for kind in ACROSS:
            weight_copy(which, me, kind).start()
        start_if(weight_copy(which, me, UP), a < major - 1)
        start_if(weight_copy(which, me, DOWN), a > 0)

    before = (
        lax.broadcasted_iota(jnp.int32, (seq, seq), 0) < lax.broadcasted_iota(jnp.int32, (seq, seq), 1)
    ).astype(jnp.float32).astype(jnp.bfloat16)

    def ranks(code, owner):
        local = code - owner * items
        mine = (local >= 0) & (local < items)
        flag = jnp.where(mine, 1.0, 0.0)
        rank = dot(flag.astype(jnp.bfloat16), before).astype(jnp.int32)
        return local, mine, rank

    def one_hot(keys, count):
        spot = lax.broadcasted_iota(jnp.int32, (count, seq), 0)
        return jnp.where(spot == keys, 1.0, 0.0)

    def answer(to):
        local, mine, rank = ranks(codes[to], me)
        slot = jnp.where(mine, rank, -1)
        pick_slot = one_hot(slot[:1], cap).astype(jnp.bfloat16)
        pick_row = one_hot(local[:1], items).astype(jnp.bfloat16)
        pick = dot(pick_slot, pick_row, (1, 1)).astype(jnp.bfloat16)
        return dot(pick, table_ref[...]).astype(jnp.bfloat16)

    found[me] = answer(me)

    def send_answer(off, _):
        to = lax.rem(me + off, groups)
        code_copy(to, to).wait_recv()
        answers[to] = answer(to)
        found_copy(to, me).start()
        return 0

    lax.fori_loop(1, groups, send_answer, 0)

    for off in range(1, minor):
        spot = other(off)
        weight_copy(1, spot, UP).wait_recv()
        start_if(weight_copy(1, spot, UP), a < major - 1)
        start_if(weight_copy(1, spot, DOWN), a > 0)

    for step in range(1, major):
        for sign, kind, inside, onward in (
            (-1, UP, a - step >= 0, a < major - 1),
            (1, DOWN, a + step < major, a > 0),
        ):
            @pl.when(inside)
            def _():
                for off in range(minor):
                    spot = (a + sign * step) * minor + (b + off) % minor
                    weight_copy(1, spot, kind).wait_recv()
                    start_if(weight_copy(1, spot, kind), onward)
                spot = (a + sign * step) * minor + b
                weight_copy(0, spot, kind).wait_recv()
                start_if(weight_copy(0, spot, kind), onward)
                for across in ACROSS:
                    weight_copy(0, spot, across).start()

    def key_of(owner, keys):
        _, mine, rank = ranks(codes[me], owner)
        return jnp.where(mine, owner * cap + rank, keys)

    keys = lax.fori_loop(0, groups, key_of, jnp.zeros((SUBLANES, seq), jnp.int32))
    place = one_hot(keys[:1], groups * cap).T.astype(jnp.bfloat16)

    def wait_found(off, _):
        source = lax.rem(me + off, groups)
        found_copy(source, source).wait_recv()
        return 0

    lax.fori_loop(1, groups, wait_found, 0)
    embedded = dot(place, found[...].reshape(groups * cap, width)).astype(jnp.bfloat16)

    @pl.when(here == 0)
    def _():
        xin[0] = embedded

    @pl.when(here > 0)
    def _():
        staged[...] = embedded
        to_first(here).start()

    for off in range(1, minor):
        for line in range(major):
            weight_copy(0, line * minor + (b + off) % minor, 1 + off).wait_recv()

    later = lax.broadcasted_iota(jnp.int32, (seq, seq), 1)
    causal = later <= lax.broadcasted_iota(jnp.int32, (seq, seq), 0)

    def layer(slot, _):
        @pl.when((here > 0) | (slot > 0))
        def _():
            to_first(slot).wait_recv()

        wide = xin[slot].astype(jnp.float32)
        normed[...] = (normalize(wide) * gain_in_ref[...]).astype(jnp.bfloat16)
        for tile in range(4 * width // (4 * head)):
            columns = slice(tile * 4 * head, (tile + 1) * 4 * head)
            uvqk[:, columns] = silu(dot(normed[...], win[:, columns])).astype(jnp.bfloat16)
        allowed = causal & (later < lens_ref[slot, 0])
        for h in range(HEADS):
            part = [slice(k * width + h * head, k * width + (h + 1) * head) for k in range(4)]
            scores = dot(uvqk[:, part[2]], uvqk[:, part[3]], (1, 1)) * (head**-0.5)
            weights = jnp.where(allowed, silu(scores), 0.0).astype(jnp.bfloat16)
            attn[:, part[0]] = dot(weights, uvqk[:, part[1]])
        mixed = normalize(attn[...]) * gain_mid_ref[...] * uvqk[:, :width].astype(jnp.float32)
        normed[...] = mixed.astype(jnp.bfloat16)
        out_ref[slot] = (dot(normed[...], wout[...]) + xin[slot].astype(jnp.float32)).astype(jnp.bfloat16)

        @pl.when(here < sections - 1)
        def _():
            to_next(slot).start()

        return 0

    lax.fori_loop(0, micro, layer, 0)

    def left(off, _):
        to = lax.rem(me + off, groups)
        code_copy(me, to).wait_send()
        found_copy(to, me).wait_send()
        return 0

    lax.fori_loop(1, groups, left, 0)
    for which in (1, 0):
        for kind in ACROSS:
            weight_copy(which, me, kind).wait_send()
    for off in range(minor):
        for which in (1, 0) if off == 0 else (1,):
            copies = [weight_copy(which, other(off), kind) for kind in (UP, DOWN)]
            pl.when(a < major - 1)(copies[0].wait_send)
            pl.when(a > 0)(copies[1].wait_send)
    for step in range(1, major):
        for sign, kind, inside, onward in (
            (-1, UP, a - step >= 0, a < major - 1),
            (1, DOWN, a + step < major, a > 0),
        ):
            @pl.when(inside)
            def _():
                for off in range(minor):
                    spot = (a + sign * step) * minor + (b + off) % minor
                    pl.when(onward)(weight_copy(1, spot, kind).wait_send)
                spot = (a + sign * step) * minor + b
                pl.when(onward)(weight_copy(0, spot, kind).wait_send)
                for across in ACROSS:
                    weight_copy(0, spot, across).wait_send()

    pl.when(here > 0)(to_first(here).wait_send)

    def passed(slot, _):
        pl.when(here < sections - 1)(to_next(slot).wait_send)
        return 0

    lax.fori_loop(0, micro, passed, 0)


def on_device(lines, item_owner, item_row, lengths, table, w_in, w_out, gain_in, gain_mid):
    major, minor = lines
    groups = major * minor
    items, width = table.shape
    seq = item_row.shape[-1]
    micro = lengths.shape[0]
    cap = max(PACKED_ROWS, 2 * seq // groups)
    code = item_owner.reshape(1, seq) * items + item_row.reshape(1, seq)
    inner = w_in.shape[1] * groups
    vmem = pl.BlockSpec(memory_space=pltpu.VMEM)
    hbm = pl.BlockSpec(memory_space=pl.ANY)
    smem = pl.BlockSpec(memory_space=pltpu.SMEM)
    dma = pltpu.SemaphoreType.DMA
    kinds = minor + 1
    bf16 = jnp.bfloat16
    out = pl.pallas_call(
        functools.partial(kernel, lines),
        out_shape=jax.ShapeDtypeStruct((micro, seq, width), bf16),
        in_specs=[smem, vmem, vmem, hbm, hbm, vmem, vmem],
        out_specs=vmem,
        scratch_shapes=[
            pltpu.VMEM((inner, w_in.shape[2]), bf16),
            pltpu.VMEM((w_out.shape[1] * groups, width), bf16),
            pltpu.VMEM((groups, SUBLANES, seq), jnp.int32),
            pltpu.VMEM((groups, cap, width), bf16),
            pltpu.VMEM((groups, cap, width), bf16),
            pltpu.VMEM((seq, width), bf16),
            pltpu.VMEM((micro, seq, width), bf16),
            pltpu.VMEM((seq, width), bf16),
            pltpu.VMEM((seq, w_in.shape[2]), bf16),
            pltpu.VMEM((seq, width), jnp.float32),
            dma((2,)),
            dma((groups, kinds)),
            dma((groups,)),
            dma((groups, kinds)),
            dma((groups,)),
            dma((groups,)),
            dma((groups,)),
            dma((groups,)),
            dma((groups,)),
            dma((1,)),
            dma((micro,)),
            dma((micro,)),
        ],
        compiler_params=pltpu.CompilerParams(
            has_side_effects=True, vmem_limit_bytes=40 * 2**20
        ),
        name="sections",
    )(lengths, code, table, w_in[0], w_out[0], gain_in, gain_mid)
    return out[None, None]


def lines_of(mesh):
    along = [device.coords for device in mesh.devices[0]]
    moved = [[axis for axis in range(3) if along[0][axis] != spot[axis]] for spot in along]
    minor = 1
    while minor < len(along) and moved[minor] == moved[1] and len(moved[1]) == 1:
        minor += 1
    return len(along) // minor, minor


def solution(mesh):
    in_specs = (
        P("section", "dp", None, None),
        P("section", "dp", None),
        P(None, "dp"),
        P("dp", None),
        P("section", "dp", None),
        P("section", "dp", None),
        P("section", None),
        P("section", None),
    )
    out_specs = P("section", "dp", None, None, None)
    return jax.shard_map(
        functools.partial(on_device, lines_of(mesh)),
        mesh=mesh, in_specs=in_specs, out_specs=out_specs, check_vma=False,
    )
```

```python
import functools

import jax
import jax.numpy as jnp
from jax import lax
from jax.experimental import pallas as pl
from jax.experimental.pallas import tpu as pltpu
from jax.sharding import PartitionSpec as P

HEADS = 8
EPS = 1e-05
MESH = pl.DeviceIdType.MESH
SUBLANES = 8
PACKED_ROWS = 16


def dot(a, b, contract=(1, 0)):
    dims = (((contract[0],), (contract[1],)), ((), ()))
    return lax.dot_general(a, b, dims, preferred_element_type=jnp.float32)


def silu(v):
    half = 0.5 * v
    return half + half * jnp.tanh(half)


def normalize(values):
    center = values - jnp.mean(values, axis=-1, keepdims=True)
    spread = jnp.mean(center * center, axis=-1, keepdims=True)
    return center * lax.rsqrt(spread + EPS)


def kernel(
    lines,
    lens_ref, code_ref, table_ref, w_in_ref, w_out_ref, gain_in_ref, gain_mid_ref,
    out_ref,
    win, wout, codes, answers, found, staged, xin, normed, uvqk, attn,
    local_sem, win_send, win_recv, wout_send, wout_recv,
    code_send, code_recv, found_send, found_recv, x_send, x_recv, next_send,
):
    major, minor = lines
    groups = major * minor
    here, me = lax.axis_index("section"), lax.axis_index("dp")
    sections = lax.axis_size("section")
    a, b = me // minor, me % minor
    depth, depth_out = w_in_ref.shape[0], w_out_ref.shape[0]
    micro, seq, width = xin.shape
    cap = answers.shape[1]
    items = table_ref.shape[0]
    pieces = win_recv.shape[0] // groups
    head = width // HEADS

    def rows(ref, block, count):
        return ref.at[pl.ds(pl.multiple_of(block * count, count), count)]

    def target(kind):
        if kind == 0:
            return (a + 1) * minor + b
        if kind == 1:
            return (a - 1) * minor + b
        return a * minor + (b + kind - 1) % minor

    def weight_copy(which, block, kind, piece=0):
        full, send, recv, count = (
            (win, win_send, win_recv, depth // pieces)
            if which == 0
            else (wout, wout_send, wout_recv, depth_out)
        )
        spot = block * pieces + piece if which == 0 else block
        part = rows(full, spot, count)
        return pltpu.make_async_remote_copy(
            src_ref=part, dst_ref=part, send_sem=send.at[spot, kind], recv_sem=recv.at[spot],
            device_id={"dp": target(kind)}, device_id_type=MESH,
        )

    def code_copy(block, to):
        return pltpu.make_async_remote_copy(
            src_ref=codes.at[block], dst_ref=codes.at[block], send_sem=code_send.at[to],
            recv_sem=code_recv.at[block], device_id={"dp": to}, device_id_type=MESH,
        )

    def found_copy(to, block):
        return pltpu.make_async_remote_copy(
            src_ref=answers.at[to], dst_ref=found.at[block], send_sem=found_send.at[to],
            recv_sem=found_recv.at[block], device_id={"dp": to}, device_id_type=MESH,
        )

    def to_first(slot):
        return pltpu.make_async_remote_copy(
            src_ref=staged, dst_ref=xin.at[slot], send_sem=x_send.at[0], recv_sem=x_recv.at[slot],
            device_id={"section": 0}, device_id_type=MESH,
        )

    def to_next(slot):
        return pltpu.make_async_remote_copy(
            src_ref=out_ref.at[slot], dst_ref=xin.at[slot], send_sem=next_send.at[slot],
            recv_sem=x_recv.at[slot], device_id={"section": here + 1}, device_id_type=MESH,
        )

    UP, DOWN = 0, 1
    ACROSS = range(2, minor + 1)

    def other(off):
        return a * minor + (b + off) % minor

    def start_if(copy, condition):
        if condition is None:
            copy.start()
        else:
            pl.when(condition)(copy.start)

    own_in = pltpu.make_async_copy(w_in_ref, rows(win, me, depth), local_sem.at[0])
    own_out = pltpu.make_async_copy(w_out_ref, rows(wout, me, depth_out), local_sem.at[1])
    own_in.start()
    own_out.start()
    codes[me] = jnp.broadcast_to(code_ref[...], codes.shape[1:])

    def send_code(off, _):
        code_copy(me, lax.rem(me + off, groups)).start()
        return 0

    lax.fori_loop(1, groups, send_code, 0)
    own_out.wait()
    own_in.wait()
    for kind in ACROSS:
        weight_copy(1, me, kind).start()
    start_if(weight_copy(1, me, UP), a < major - 1)
    start_if(weight_copy(1, me, DOWN), a > 0)

    def send_own(piece, _):
        start_if(weight_copy(0, me, UP, piece), a < major - 1)
        start_if(weight_copy(0, me, DOWN, piece), a > 0)
        for kind in ACROSS:
            weight_copy(0, me, kind, piece).start()
        return 0

    lax.fori_loop(0, pieces, send_own, 0)

    before = (
        lax.broadcasted_iota(jnp.int32, (seq, seq), 0) < lax.broadcasted_iota(jnp.int32, (seq, seq), 1)
    ).astype(jnp.float32).astype(jnp.bfloat16)

    def ranks(code, owner):
        local = code - owner * items
        mine = (local >= 0) & (local < items)
        flag = jnp.where(mine, 1.0, 0.0)
        rank = dot(flag.astype(jnp.bfloat16), before).astype(jnp.int32)
        return local, mine, rank

    def one_hot(keys, count):
        spot = lax.broadcasted_iota(jnp.int32, (count, seq), 0)
        return jnp.where(spot == keys, 1.0, 0.0)

    def answer(to):
        local, mine, rank = ranks(codes[to], me)
        slot = jnp.where(mine, rank, -1)
        pick_slot = one_hot(slot[:1], cap).astype(jnp.bfloat16)
        pick_row = one_hot(local[:1], items).astype(jnp.bfloat16)
        pick = dot(pick_slot, pick_row, (1, 1)).astype(jnp.bfloat16)
        return dot(pick, table_ref[...]).astype(jnp.bfloat16)

    found[me] = answer(me)

    def send_answer(off, _):
        to = lax.rem(me + off, groups)
        code_copy(to, to).wait_recv()
        answers[to] = answer(to)
        found_copy(to, me).start()
        return 0

    lax.fori_loop(1, groups, send_answer, 0)

    for off in range(1, minor):
        spot = other(off)
        weight_copy(1, spot, UP).wait_recv()
        start_if(weight_copy(1, spot, UP), a < major - 1)
        start_if(weight_copy(1, spot, DOWN), a > 0)

    def sides(step):
        return (
            (-step, UP, a - step >= 0, a < major - 1),
            (step, DOWN, a + step < major, a > 0),
        )

    for step in range(1, major):
        for shift, kind, inside, onward in sides(step):
            @pl.when(inside)
            def _():
                for off in range(minor):
                    spot = (a + shift) * minor + (b + off) % minor
                    weight_copy(1, spot, kind).wait_recv()
                    start_if(weight_copy(1, spot, kind), onward)

        def relay(piece, _):
            for shift, kind, inside, onward in sides(step):
                @pl.when(inside)
                def _():
                    spot = (a + shift) * minor + b
                    weight_copy(0, spot, kind, piece).wait_recv()
                    start_if(weight_copy(0, spot, kind, piece), onward)
                    for across in ACROSS:
                        weight_copy(0, spot, across, piece).start()

            return 0

        lax.fori_loop(0, pieces, relay, 0)

    def key_of(owner, keys):
        _, mine, rank = ranks(codes[me], owner)
        return jnp.where(mine, owner * cap + rank, keys)

    keys = lax.fori_loop(0, groups, key_of, jnp.zeros((SUBLANES, seq), jnp.int32))
    place = one_hot(keys[:1], groups * cap).T.astype(jnp.bfloat16)

    def wait_found(off, _):
        source = lax.rem(me + off, groups)
        found_copy(source, source).wait_recv()
        return 0

    lax.fori_loop(1, groups, wait_found, 0)
    embedded = dot(place, found[...].reshape(groups * cap, width)).astype(jnp.bfloat16)

    @pl.when(here == 0)
    def _():
        xin[0] = embedded

    @pl.when(here > 0)
    def _():
        staged[...] = embedded
        to_first(here).start()

    for off in range(1, minor):
        def arrived(count, _):
            line, piece = count // pieces, count % pieces
            weight_copy(0, line * minor + (b + off) % minor, 1 + off, piece).wait_recv()
            return 0

        lax.fori_loop(0, major * pieces, arrived, 0)

    later = lax.broadcasted_iota(jnp.int32, (seq, seq), 1)
    causal = later <= lax.broadcasted_iota(jnp.int32, (seq, seq), 0)

    def layer(slot, _):
        @pl.when((here > 0) | (slot > 0))
        def _():
            to_first(slot).wait_recv()

        wide = xin[slot].astype(jnp.float32)
        normed[...] = (normalize(wide) * gain_in_ref[...]).astype(jnp.bfloat16)
        for tile in range(4 * width // (4 * head)):
            columns = slice(tile * 4 * head, (tile + 1) * 4 * head)
            uvqk[:, columns] = silu(dot(normed[...], win[:, columns])).astype(jnp.bfloat16)
        allowed = causal & (later < lens_ref[slot, 0])
        for h in range(HEADS):
            part = [slice(k * width + h * head, k * width + (h + 1) * head) for k in range(4)]
            scores = dot(uvqk[:, part[2]], uvqk[:, part[3]], (1, 1)) * (head**-0.5)
            weights = jnp.where(allowed, silu(scores), 0.0).astype(jnp.bfloat16)
            attn[:, part[0]] = dot(weights, uvqk[:, part[1]])
        mixed = normalize(attn[...]) * gain_mid_ref[...] * uvqk[:, :width].astype(jnp.float32)
        normed[...] = mixed.astype(jnp.bfloat16)
        out_ref[slot] = (dot(normed[...], wout[...]) + xin[slot].astype(jnp.float32)).astype(jnp.bfloat16)

        @pl.when(here < sections - 1)
        def _():
            to_next(slot).start()

        return 0

    lax.fori_loop(0, micro, layer, 0)

    def left(off, _):
        to = lax.rem(me + off, groups)
        code_copy(me, to).wait_send()
        found_copy(to, me).wait_send()
        return 0

    lax.fori_loop(1, groups, left, 0)
    for kind in ACROSS:
        weight_copy(1, me, kind).wait_send()
    for off in range(minor):
        pl.when(a < major - 1)(weight_copy(1, other(off), UP).wait_send)
        pl.when(a > 0)(weight_copy(1, other(off), DOWN).wait_send)

    def own_left(piece, _):
        pl.when(a < major - 1)(weight_copy(0, me, UP, piece).wait_send)
        pl.when(a > 0)(weight_copy(0, me, DOWN, piece).wait_send)
        for kind in ACROSS:
            weight_copy(0, me, kind, piece).wait_send()
        return 0

    lax.fori_loop(0, pieces, own_left, 0)
    for step in range(1, major):
        for shift, kind, inside, onward in sides(step):
            @pl.when(inside)
            def _():
                for off in range(minor):
                    spot = (a + shift) * minor + (b + off) % minor
                    pl.when(onward)(weight_copy(1, spot, kind).wait_send)

                def relay_left(piece, _):
                    spot = (a + shift) * minor + b
                    pl.when(onward)(weight_copy(0, spot, kind, piece).wait_send)
                    for across in ACROSS:
                        weight_copy(0, spot, across, piece).wait_send()
                    return 0

                lax.fori_loop(0, pieces, relay_left, 0)

    pl.when(here > 0)(to_first(here).wait_send)

    def passed(slot, _):
        pl.when(here < sections - 1)(to_next(slot).wait_send)
        return 0

    lax.fori_loop(0, micro, passed, 0)


def on_device(lines, item_owner, item_row, lengths, table, w_in, w_out, gain_in, gain_mid):
    major, minor = lines
    groups = major * minor
    items, width = table.shape
    seq = item_row.shape[-1]
    micro = lengths.shape[0]
    cap = max(PACKED_ROWS, 2 * seq // groups)
    code = item_owner.reshape(1, seq) * items + item_row.reshape(1, seq)
    inner = w_in.shape[1] * groups
    vmem = pl.BlockSpec(memory_space=pltpu.VMEM)
    hbm = pl.BlockSpec(memory_space=pl.ANY)
    smem = pl.BlockSpec(memory_space=pltpu.SMEM)
    dma = pltpu.SemaphoreType.DMA
    kinds = minor + 1
    pieces = max(1, w_in.shape[1] // (2 * PACKED_ROWS))
    bf16 = jnp.bfloat16
    out = pl.pallas_call(
        functools.partial(kernel, lines),
        out_shape=jax.ShapeDtypeStruct((micro, seq, width), bf16),
        in_specs=[smem, vmem, vmem, hbm, hbm, vmem, vmem],
        out_specs=vmem,
        scratch_shapes=[
            pltpu.VMEM((inner, w_in.shape[2]), bf16),
            pltpu.VMEM((w_out.shape[1] * groups, width), bf16),
            pltpu.VMEM((groups, SUBLANES, seq), jnp.int32),
            pltpu.VMEM((groups, cap, width), bf16),
            pltpu.VMEM((groups, cap, width), bf16),
            pltpu.VMEM((seq, width), bf16),
            pltpu.VMEM((micro, seq, width), bf16),
            pltpu.VMEM((seq, width), bf16),
            pltpu.VMEM((seq, w_in.shape[2]), bf16),
            pltpu.VMEM((seq, width), jnp.float32),
            dma((2,)),
            dma((groups * pieces, kinds)),
            dma((groups * pieces,)),
            dma((groups, kinds)),
            dma((groups,)),
            dma((groups,)),
            dma((groups,)),
            dma((groups,)),
            dma((groups,)),
            dma((1,)),
            dma((micro,)),
            dma((micro,)),
        ],
        compiler_params=pltpu.CompilerParams(
            has_side_effects=True, vmem_limit_bytes=40 * 2**20
        ),
        name="sections",
    )(lengths, code, table, w_in[0], w_out[0], gain_in, gain_mid)
    return out[None, None]


def lines_of(mesh):
    along = [device.coords for device in mesh.devices[0]]
    moved = [[axis for axis in range(3) if along[0][axis] != spot[axis]] for spot in along]
    minor = 1
    while minor < len(along) and moved[minor] == moved[1] and len(moved[1]) == 1:
        minor += 1
    return len(along) // minor, minor


def solution(mesh):
    in_specs = (
        P("section", "dp", None, None),
        P("section", "dp", None),
        P(None, "dp"),
        P("dp", None),
        P("section", "dp", None),
        P("section", "dp", None),
        P("section", None),
        P("section", None),
    )
    out_specs = P("section", "dp", None, None, None)
    return jax.shard_map(
        functools.partial(on_device, lines_of(mesh)),
        mesh=mesh, in_specs=in_specs, out_specs=out_specs, check_vma=False,
    )
```

```python
import functools

import jax
import jax.numpy as jnp
from jax import lax
from jax.experimental import pallas as pl
from jax.experimental.pallas import tpu as pltpu
from jax.sharding import PartitionSpec as P

HEADS = 8
EPS = 1e-05
MESH = pl.DeviceIdType.MESH
SUBLANES = 8
PACKED_ROWS = 16


def dot(a, b, contract=(1, 0)):
    dims = (((contract[0],), (contract[1],)), ((), ()))
    return lax.dot_general(a, b, dims, preferred_element_type=jnp.float32)


def silu(v):
    half = 0.5 * v
    return half + half * jnp.tanh(half)


def normalize(values):
    center = values - jnp.mean(values, axis=-1, keepdims=True)
    spread = jnp.mean(center * center, axis=-1, keepdims=True)
    return center * lax.rsqrt(spread + EPS)


def kernel(
    lines,
    lens_ref, code_ref, table_ref, w_in_ref, w_out_ref, gain_in_ref, gain_mid_ref,
    out_ref,
    win, wout, codes, answers, found, staged, xin, normed, uvqk, attn,
    local_sem, win_send, win_recv, wout_send, wout_recv,
    code_send, code_recv, found_send, found_recv, x_send, x_recv, next_send,
):
    major, minor = lines
    groups = major * minor
    here, me = lax.axis_index("section"), lax.axis_index("dp")
    sections = lax.axis_size("section")
    a, b = me // minor, me % minor
    depth, depth_out = w_in_ref.shape[0], w_out_ref.shape[0]
    micro, seq, width = xin.shape
    cap = answers.shape[1]
    items = table_ref.shape[0]
    pieces = win_recv.shape[0] // groups
    head = width // HEADS

    def rows(ref, block, count):
        return ref.at[pl.ds(pl.multiple_of(block * count, count), count)]

    def target(kind):
        if kind == 0:
            return (a + 1) * minor + b
        if kind == 1:
            return (a - 1) * minor + b
        return a * minor + (b + kind - 1) % minor

    def weight_copy(which, block, kind, piece=0):
        full, send, recv, count = (
            (win, win_send, win_recv, depth // pieces)
            if which == 0
            else (wout, wout_send, wout_recv, depth_out)
        )
        spot = block * pieces + piece if which == 0 else block
        part = rows(full, spot, count)
        return pltpu.make_async_remote_copy(
            src_ref=part, dst_ref=part, send_sem=send.at[spot, kind], recv_sem=recv.at[spot],
            device_id={"dp": target(kind)}, device_id_type=MESH,
        )

    def code_copy(block, to):
        return pltpu.make_async_remote_copy(
            src_ref=codes.at[block], dst_ref=codes.at[block], send_sem=code_send.at[to],
            recv_sem=code_recv.at[block], device_id={"dp": to}, device_id_type=MESH,
        )

    def found_copy(to, block):
        return pltpu.make_async_remote_copy(
            src_ref=answers.at[to], dst_ref=found.at[block], send_sem=found_send.at[to],
            recv_sem=found_recv.at[block], device_id={"dp": to}, device_id_type=MESH,
        )

    def to_first(slot):
        return pltpu.make_async_remote_copy(
            src_ref=staged, dst_ref=xin.at[slot], send_sem=x_send.at[0], recv_sem=x_recv.at[slot],
            device_id={"section": 0}, device_id_type=MESH,
        )

    def to_next(slot):
        return pltpu.make_async_remote_copy(
            src_ref=out_ref.at[slot], dst_ref=xin.at[slot], send_sem=next_send.at[slot],
            recv_sem=x_recv.at[slot], device_id={"section": here + 1}, device_id_type=MESH,
        )

    UP, DOWN = 0, 1
    ACROSS = range(2, minor + 1)

    def other(off):
        return a * minor + (b + off) % minor

    def start_if(copy, condition):
        if condition is None:
            copy.start()
        else:
            pl.when(condition)(copy.start)

    own_in = pltpu.make_async_copy(w_in_ref, rows(win, me, depth), local_sem.at[0])
    own_out = pltpu.make_async_copy(w_out_ref, rows(wout, me, depth_out), local_sem.at[1])
    own_in.start()
    own_out.start()
    codes[me] = jnp.broadcast_to(code_ref[...], codes.shape[1:])

    def send_code(off, _):
        code_copy(me, lax.rem(me + off, groups)).start()
        return 0

    lax.fori_loop(1, groups, send_code, 0)
    own_out.wait()
    own_in.wait()
    for kind in ACROSS:
        weight_copy(1, me, kind).start()

    def send_own(piece, _):
        start_if(weight_copy(0, me, UP, piece), a < major - 1)
        start_if(weight_copy(0, me, DOWN, piece), a > 0)
        for kind in ACROSS:
            weight_copy(0, me, kind, piece).start()
        return 0

    lax.fori_loop(0, pieces, send_own, 0)
    start_if(weight_copy(1, me, UP), a < major - 1)
    start_if(weight_copy(1, me, DOWN), a > 0)

    before = (
        lax.broadcasted_iota(jnp.int32, (seq, seq), 0) < lax.broadcasted_iota(jnp.int32, (seq, seq), 1)
    ).astype(jnp.float32).astype(jnp.bfloat16)

    def ranks(code, owner):
        local = code - owner * items
        mine = (local >= 0) & (local < items)
        flag = jnp.where(mine, 1.0, 0.0)
        rank = dot(flag.astype(jnp.bfloat16), before).astype(jnp.int32)
        return local, mine, rank

    def one_hot(keys, count):
        spot = lax.broadcasted_iota(jnp.int32, (count, seq), 0)
        return jnp.where(spot == keys, 1.0, 0.0)

    def answer(to):
        local, mine, rank = ranks(codes[to], me)
        slot = jnp.where(mine, rank, -1)
        pick_slot = one_hot(slot[:1], cap).astype(jnp.bfloat16)
        pick_row = one_hot(local[:1], items).astype(jnp.bfloat16)
        pick = dot(pick_slot, pick_row, (1, 1)).astype(jnp.bfloat16)
        return dot(pick, table_ref[...]).astype(jnp.bfloat16)

    found[me] = answer(me)

    def send_answer(off, _):
        to = lax.rem(me + off, groups)
        code_copy(to, to).wait_recv()
        answers[to] = answer(to)
        found_copy(to, me).start()
        return 0

    lax.fori_loop(1, groups, send_answer, 0)

    for off in range(1, minor):
        spot = other(off)
        weight_copy(1, spot, UP).wait_recv()
        start_if(weight_copy(1, spot, UP), a < major - 1)
        start_if(weight_copy(1, spot, DOWN), a > 0)

    def sides(step):
        return (
            (-step, UP, a - step >= 0, a < major - 1),
            (step, DOWN, a + step < major, a > 0),
        )

    for step in range(1, major):
        def relay(piece, _):
            for shift, kind, inside, onward in sides(step):
                @pl.when(inside)
                def _():
                    spot = (a + shift) * minor + b
                    weight_copy(0, spot, kind, piece).wait_recv()
                    start_if(weight_copy(0, spot, kind, piece), onward)
                    for across in ACROSS:
                        weight_copy(0, spot, across, piece).start()

            return 0

        lax.fori_loop(0, pieces, relay, 0)
        for shift, kind, inside, onward in sides(step):
            @pl.when(inside)
            def _():
                for off in range(minor):
                    spot = (a + shift) * minor + (b + off) % minor
                    weight_copy(1, spot, kind).wait_recv()
                    start_if(weight_copy(1, spot, kind), onward)

    def key_of(owner, keys):
        _, mine, rank = ranks(codes[me], owner)
        return jnp.where(mine, owner * cap + rank, keys)

    keys = lax.fori_loop(0, groups, key_of, jnp.zeros((SUBLANES, seq), jnp.int32))
    place = one_hot(keys[:1], groups * cap).T.astype(jnp.bfloat16)

    def wait_found(off, _):
        source = lax.rem(me + off, groups)
        found_copy(source, source).wait_recv()
        return 0

    lax.fori_loop(1, groups, wait_found, 0)
    embedded = dot(place, found[...].reshape(groups * cap, width)).astype(jnp.bfloat16)

    @pl.when(here == 0)
    def _():
        xin[0] = embedded

    @pl.when(here > 0)
    def _():
        staged[...] = embedded
        to_first(here).start()

    for off in range(1, minor):
        def arrived(count, _):
            line, piece = count // pieces, count % pieces
            weight_copy(0, line * minor + (b + off) % minor, 1 + off, piece).wait_recv()
            return 0

        lax.fori_loop(0, major * pieces, arrived, 0)

    later = lax.broadcasted_iota(jnp.int32, (seq, seq), 1)
    causal = later <= lax.broadcasted_iota(jnp.int32, (seq, seq), 0)

    def layer(slot, _):
        @pl.when((here > 0) | (slot > 0))
        def _():
            to_first(slot).wait_recv()

        wide = xin[slot].astype(jnp.float32)
        normed[...] = (normalize(wide) * gain_in_ref[...]).astype(jnp.bfloat16)
        for tile in range(4 * width // (4 * head)):
            columns = slice(tile * 4 * head, (tile + 1) * 4 * head)
            uvqk[:, columns] = silu(dot(normed[...], win[:, columns])).astype(jnp.bfloat16)
        allowed = causal & (later < lens_ref[slot, 0])
        for h in range(HEADS):
            part = [slice(k * width + h * head, k * width + (h + 1) * head) for k in range(4)]
            scores = dot(uvqk[:, part[2]], uvqk[:, part[3]], (1, 1)) * (head**-0.5)
            weights = jnp.where(allowed, silu(scores), 0.0).astype(jnp.bfloat16)
            attn[:, part[0]] = dot(weights, uvqk[:, part[1]])
        mixed = normalize(attn[...]) * gain_mid_ref[...] * uvqk[:, :width].astype(jnp.float32)
        normed[...] = mixed.astype(jnp.bfloat16)
        out_ref[slot] = (dot(normed[...], wout[...]) + xin[slot].astype(jnp.float32)).astype(jnp.bfloat16)

        @pl.when(here < sections - 1)
        def _():
            to_next(slot).start()

        return 0

    lax.fori_loop(0, micro, layer, 0)

    def left(off, _):
        to = lax.rem(me + off, groups)
        code_copy(me, to).wait_send()
        found_copy(to, me).wait_send()
        return 0

    lax.fori_loop(1, groups, left, 0)
    for kind in ACROSS:
        weight_copy(1, me, kind).wait_send()
    for off in range(minor):
        pl.when(a < major - 1)(weight_copy(1, other(off), UP).wait_send)
        pl.when(a > 0)(weight_copy(1, other(off), DOWN).wait_send)

    def own_left(piece, _):
        pl.when(a < major - 1)(weight_copy(0, me, UP, piece).wait_send)
        pl.when(a > 0)(weight_copy(0, me, DOWN, piece).wait_send)
        for kind in ACROSS:
            weight_copy(0, me, kind, piece).wait_send()
        return 0

    lax.fori_loop(0, pieces, own_left, 0)
    for step in range(1, major):
        for shift, kind, inside, onward in sides(step):
            @pl.when(inside)
            def _():
                for off in range(minor):
                    spot = (a + shift) * minor + (b + off) % minor
                    pl.when(onward)(weight_copy(1, spot, kind).wait_send)

                def relay_left(piece, _):
                    spot = (a + shift) * minor + b
                    pl.when(onward)(weight_copy(0, spot, kind, piece).wait_send)
                    for across in ACROSS:
                        weight_copy(0, spot, across, piece).wait_send()
                    return 0

                lax.fori_loop(0, pieces, relay_left, 0)

    pl.when(here > 0)(to_first(here).wait_send)

    def passed(slot, _):
        pl.when(here < sections - 1)(to_next(slot).wait_send)
        return 0

    lax.fori_loop(0, micro, passed, 0)


def on_device(lines, item_owner, item_row, lengths, table, w_in, w_out, gain_in, gain_mid):
    major, minor = lines
    groups = major * minor
    items, width = table.shape
    seq = item_row.shape[-1]
    micro = lengths.shape[0]
    cap = max(PACKED_ROWS, 2 * seq // groups)
    code = item_owner.reshape(1, seq) * items + item_row.reshape(1, seq)
    inner = w_in.shape[1] * groups
    vmem = pl.BlockSpec(memory_space=pltpu.VMEM)
    hbm = pl.BlockSpec(memory_space=pl.ANY)
    smem = pl.BlockSpec(memory_space=pltpu.SMEM)
    dma = pltpu.SemaphoreType.DMA
    kinds = minor + 1
    pieces = max(1, w_in.shape[1] // (2 * PACKED_ROWS))
    bf16 = jnp.bfloat16
    out = pl.pallas_call(
        functools.partial(kernel, lines),
        out_shape=jax.ShapeDtypeStruct((micro, seq, width), bf16),
        in_specs=[smem, vmem, vmem, hbm, hbm, vmem, vmem],
        out_specs=vmem,
        scratch_shapes=[
            pltpu.VMEM((inner, w_in.shape[2]), bf16),
            pltpu.VMEM((w_out.shape[1] * groups, width), bf16),
            pltpu.VMEM((groups, SUBLANES, seq), jnp.int32),
            pltpu.VMEM((groups, cap, width), bf16),
            pltpu.VMEM((groups, cap, width), bf16),
            pltpu.VMEM((seq, width), bf16),
            pltpu.VMEM((micro, seq, width), bf16),
            pltpu.VMEM((seq, width), bf16),
            pltpu.VMEM((seq, w_in.shape[2]), bf16),
            pltpu.VMEM((seq, width), jnp.float32),
            dma((2,)),
            dma((groups * pieces, kinds)),
            dma((groups * pieces,)),
            dma((groups, kinds)),
            dma((groups,)),
            dma((groups,)),
            dma((groups,)),
            dma((groups,)),
            dma((groups,)),
            dma((1,)),
            dma((micro,)),
            dma((micro,)),
        ],
        compiler_params=pltpu.CompilerParams(
            has_side_effects=True, vmem_limit_bytes=40 * 2**20
        ),
        name="sections",
    )(lengths, code, table, w_in[0], w_out[0], gain_in, gain_mid)
    return out[None, None]


def lines_of(mesh):
    along = [device.coords for device in mesh.devices[0]]
    moved = [[axis for axis in range(3) if along[0][axis] != spot[axis]] for spot in along]
    minor = 1
    while minor < len(along) and moved[minor] == moved[1] and len(moved[1]) == 1:
        minor += 1
    return len(along) // minor, minor


def solution(mesh):
    in_specs = (
        P("section", "dp", None, None),
        P("section", "dp", None),
        P(None, "dp"),
        P("dp", None),
        P("section", "dp", None),
        P("section", "dp", None),
        P("section", None),
        P("section", None),
    )
    out_specs = P("section", "dp", None, None, None)
    return jax.shard_map(
        functools.partial(on_device, lines_of(mesh)),
        mesh=mesh, in_specs=in_specs, out_specs=out_specs, check_vma=False,
    )
```
